512 devices in a mesh: row: 4 (over x), col: 16 (over y, core), layer: 8 (over z).
Axes of the slice: x: 4, y: 8, z: 8, core: 2. Of those that a mesh axis runs over, the one named last changes fastest.
Arguments:
- iterate_rows: bfloat16 [8, 8192, 8192], P('layer', 'col', 'row'), may hold values from -0.078125 to 0.078125
- square_slab: bfloat16 [8, 8192, 2048], P('layer', 'col', 'row'), may hold values from -1 to 1
- row_pattern: int32 [8, 16, 16], P('layer', 'col'), may hold values from 0 to 1, as said below
- slab_pattern: int32 [8, 16, 4], P('layer', 'col', 'row'), may hold values 0 or 1
- fill_counts: int32 [8, 16], P('layer', 'col'), may hold values from 256 to 512
- iterate_slab: float32 [8192, 2048], P(('col', 'layer'), 'row'), may hold values from -2.5 to 2.5
Outputs:
- updated: float32 [8192, 2048], P(('col', 'layer'), 'row')
The draws below stay inside these ranges and needn't reach their ends.
Inputs may be any that keep to these rules, and one draw needn't show every extreme that they name: `row_pattern`: each aligned run of 4 tiles along the last dimension holds 0 to 2 occupied tiles; for every layer and tile row one run holds exactly 2.
All inputs are finite; a program needn't handle non-finite values. No bound on the sum of `slab_pattern` on one device may be relied on, other than what follows from the above.
Results may differ from the reference program's by a relative error of at most 0.0003.
Values may be sent and summed in bfloat16 or wider, within the bound.
A program may use at most 64 MiB of HBM per device.

```python
import jax
import jax.numpy as jnp
from jax import lax

TILE = 512
KTILES = 16
KI = 8192
PER_BLOCK = 4
CAPACITY = 2
M = 8192
N = 2048
N_ROW = 4
N_COL = 16
N_LAYER = 8


def draw_row_pattern(key, part):
    key = jax.random.fold_in(key, 11)
    key_count, key_full, key_order = jax.random.split(key, 3)
    runs = KTILES // PER_BLOCK
    counts = jax.random.randint(key_count, (N_LAYER, N_COL, runs), 0, CAPACITY + 1)
    fullest = jax.random.randint(key_full, (N_LAYER, N_COL, 1), 0, runs)
    counts = jnp.where(jnp.arange(runs, dtype=jnp.int32)[None, None, :] == fullest, CAPACITY, counts)
    scores = jax.random.randint(key_order, (N_LAYER, N_COL, runs, PER_BLOCK), 0, 1 << 20)
    scores = scores * PER_BLOCK + jnp.arange(PER_BLOCK, dtype=jnp.int32)
    ranks = jnp.argsort(jnp.argsort(scores, axis=-1), axis=-1)
    occupied = (ranks < counts[..., None]).astype(jnp.int32)
    return occupied.reshape(N_LAYER, N_COL, KTILES)


def touch_ends(drawn, key, least, largest):
    place = [jax.random.randint(jax.random.fold_in(key, axis), (), 0, length) for axis, length in enumerate(drawn.shape)]
    longest = drawn.shape.index(max(drawn.shape))
    neighbour = place[:longest] + [(place[longest] + 1) % drawn.shape[longest]] + place[longest + 1:]
    return drawn.at[tuple(place)].set(least).at[tuple(neighbour)].set(largest)


def levels(key, extent, pieces, smallest, high):
    def one(position, blocks):
        heights = jax.random.uniform(jax.random.fold_in(jax.random.fold_in(key, 6), position), (blocks,), jnp.float32, smallest / len(pieces), high / len(pieces))
        return jnp.repeat(jnp.exp(heights), extent[position] // blocks).reshape((-1,) + (1,) * (len(extent) - position - 1))

    loudness = one(*pieces[0])
    for cut in pieces[1:]:
        loudness = loudness * one(*cut)
    return loudness


def scatter_about(stream_key, dims, deviation, most, shards=(), held_as=jnp.bfloat16):
    values = jax.random.normal(stream_key, dims, jnp.float32) * deviation
    if len(shards) > 0:
        values = levels(stream_key, dims, shards, -0.22, 0.18) * values
    return jnp.clip(values, min=-most, max=most).astype(held_as)


def setup_inputs(seed: int = 0) -> dict:
    key_list = jax.random.split(jax.random.key(seed), 7)
    return {
        "iterate_rows": scatter_about(key_list[0], (N_LAYER, M, KI), (N_LAYER * KI // 12) ** -0.5, 0.078125, ((0, 8), (1, 16), (2, 4))),
        "square_slab": jnp.clip(jax.random.uniform(key_list[1], (N_LAYER, KI, N), jnp.float32, -1.0, 1.0) * levels(key_list[1], (N_LAYER, KI, N), ((0, 8), (1, 16), (2, 4)), -0.4, 0.0), -1.0, 1.0).astype(jnp.bfloat16),
        "row_pattern": draw_row_pattern(jax.random.fold_in(key_list[6], 71), 0),
        "slab_pattern": touch_ends((jax.random.randint(key_list[3], (N_LAYER, KTILES, N_ROW), 0, 3) < 2).astype(jnp.int32), jax.random.fold_in(key_list[3], 1), 0, 1),
        "fill_counts": touch_ends(jax.random.randint(key_list[4], (N_LAYER, KTILES), TILE // 2, TILE + 1), jax.random.fold_in(key_list[4], 1), TILE // 2, TILE).astype(jnp.int32),
        "iterate_slab": scatter_about(key_list[5], (M, N), 0.35, 2.5, ((0, 128), (1, 4)), jnp.float32),
    }


def expand(pattern):
    return jnp.repeat(jnp.repeat(pattern, TILE, axis=0), TILE, axis=1)


def reference(iterate_rows, square_slab, row_pattern, slab_pattern, fill_counts, iterate_slab):
    offsets = jnp.arange(TILE, dtype=jnp.int32)

    def layer_term(index):
        row_mask = expand(row_pattern[index]).astype(jnp.bfloat16)
        live = (offsets[None, :] < fill_counts[index][:, None]).reshape(KI).astype(jnp.bfloat16)
        slab_mask = expand(slab_pattern[index]).astype(jnp.bfloat16) * live[:, None]
        left = iterate_rows[index] * row_mask
        right = square_slab[index] * slab_mask
        return jnp.dot(left, right, preferred_element_type=jnp.float32)

    def accumulate(total, index):
        return total + layer_term(index), index

    product, unused = lax.scan(accumulate, jnp.zeros((M, N), jnp.float32), jnp.arange(N_LAYER, dtype=jnp.int32))
    return 1.5 * iterate_slab - 0.5 * product
```

```python
import functools

import jax
import jax.numpy as jnp
from jax import lax
from jax.experimental import pallas as pl
from jax.experimental.pallas import tpu as pltpu
from jax.sharding import PartitionSpec as P

MESH = pl.DeviceIdType.MESH
TILE = 512
RUNS = 4
PER_RUN = 4
SLOTS = 2
TILES = 16
CHIPS = 8
LAYERS = 8
CHUNKS = 4
LANES = TILE // CHUNKS
SUBS = 2
DEPTH = TILE // SUBS
STAGES = 4
OWNED = TILE // LAYERS
STAGE_ROWS = TILE // STAGES
OFFSETS = (4, 3, 5, 2, 6, 1, 7, 0)
HOPS = {("R", 0): 4, ("R", 1): 3, ("L", 0): 3, ("L", 1): 4}

SLOT_US = 1.4
LATENCY_US = 2.0
STAGE_US = 8.0


def ring_order(direction):
    streams = [(q, s) for q in range(CHUNKS) for s in range(SUBS)]
    done = {u: 0 for u in streams}
    ready = {u: 0 for u in streams}
    order, slot = [], 0
    while any(done[u] < HOPS[direction, u[1]] for u in streams):
        left = [u for u in streams if done[u] < HOPS[direction, u[1]]]
        active = [u for u in left if ready[u] <= slot]
        if active:
            u = active[0]
            done[u] += 1
            ready[u] = slot + 3
            order.append((slot, u[0], u[1], done[u]))
        slot += 1
    return order


def build_events():
    events = []
    arrival = {}
    last = [0.0] * CHUNKS
    for direction in ("R", "L"):
        for slot, q, s, hop in ring_order(direction):
            start = slot * SLOT_US
            events.append((start - SLOT_US, 1, ("send", direction, q, s, hop)))
            arrival[direction, q, s, hop] = start + SLOT_US + LATENCY_US
    for (direction, q, s, hop), when in arrival.items():
        last[q] = max(last[q], when)
        if hop == HOPS[direction, s]:
            events.append((when, 0, ("land", direction, q, s, hop)))
    for q in range(CHUNKS):
        events.append((q * 8 * SLOT_US - SLOT_US, 2, ("share", q)))
    for h in range(STAGES):
        events.append(((h - 1.5) * STAGE_US, 3, ("left", h)))
    for q in range(CHUNKS):
        for h in range(STAGES):
            when = max(last[q] + 1.0, (h + 1) * STAGE_US + LATENCY_US)
            events.append((when, 4, ("block", q, h)))
    order = sorted(events, key=lambda e: (max(e[0], 0.0), e[1], e[0]))
    return [e[2] for e in order]


def kernel(
    rows_hbm, slab_hbm, pattern_hbm, kept_hbm, fill_hbm, out_ref,
    rows, slab, pattern, kept, fill, left, right0, right1, right2, right3, partial, landed,
    in_sem, scalar_sem, left_send, left_recv, ring_send, ring_recv, pair_send, pair_recv, sum_send, sum_recv,
):
    right = (right0, right1, right2, right3)
    r, c, l = (lax.axis_index(name) for name in ("row", "col", "layer"))
    core = lax.rem(c, 2)
    sibling = (r, c + 1 - 2 * core, l)
    ring = {"R": (r, lax.rem(c + 2, TILES), l), "L": (r, lax.rem(c + TILES - 2, TILES), l)}
    row_mates = [(lax.rem(r + o, RUNS), c, l) for o in range(1, RUNS)]
    layer_mates = [(r, c, lax.rem(l + o, LAYERS)) for o in OFFSETS[:-1]]

    slab_copy = pltpu.make_async_copy(slab_hbm.at[0], slab, in_sem.at[PER_RUN])
    scalar_copies = [
        pltpu.make_async_copy(pattern_hbm, pattern, scalar_sem.at[0]),
        pltpu.make_async_copy(kept_hbm, kept, scalar_sem.at[1]),
        pltpu.make_async_copy(fill_hbm, fill, scalar_sem.at[2]),
    ]
    tile_copies = [
        pltpu.make_async_copy(rows_hbm.at[0, :, pl.ds(t * TILE, TILE)], rows.at[t], in_sem.at[t])
        for t in range(PER_RUN)
    ]
    for copy in scalar_copies + [slab_copy] + tile_copies:
        copy.start()

    barrier = pltpu.get_barrier_semaphore()
    mates = layer_mates + row_mates + [ring["R"], ring["L"], sibling]
    for mate in mates:
        pl.semaphore_signal(barrier, inc=1, device_id=mate, device_id_type=MESH)

    for copy in scalar_copies:
        copy.wait()
    picks = []
    for g in range(RUNS):
        bits = [pattern[0, 0, g * PER_RUN + t] > 0 for t in range(PER_RUN)]
        first = jnp.where(bits[0], 0, jnp.where(bits[1], 1, jnp.where(bits[2], 2, 3)))
        final = jnp.where(bits[3], 3, jnp.where(bits[2], 2, jnp.where(bits[1], 1, 0)))
        picks.append((g * PER_RUN + first, g * PER_RUN + final))
    own = [pattern[0, 0, r * PER_RUN + t] for t in range(PER_RUN)]
    count = own[0] + own[1] + own[2] + own[3]
    own_first = jnp.where(own[0] > 0, 0, jnp.where(own[1] > 0, 1, jnp.where(own[2] > 0, 2, 3)))
    own_final = jnp.where(own[3] > 0, 3, jnp.where(own[2] > 0, 2, jnp.where(own[1] > 0, 1, 0)))

    slab_copy.wait()
    limit = jnp.where(kept[0, 0, 0] > 0, fill[0, 0], 0)
    live = lax.broadcasted_iota(jnp.int32, (TILE, LANES), 0) < limit
    for q in range(CHUNKS):
        piece = slab[:, q * LANES:(q + 1) * LANES].astype(jnp.float32)
        right[q][c] = jnp.where(live, piece, 0.0).astype(jnp.bfloat16)

    for copy in tile_copies:
        copy.wait()
    for slot, (tile, least) in enumerate(((own_first, 1), (own_final, 2))):
        weight = jnp.full((OWNED, TILE), jnp.where(count >= least, 1.0, 0.0), jnp.float32).astype(jnp.bfloat16)
        for p, o in enumerate(OFFSETS):
            first_row = pl.multiple_of(lax.rem(l + o, LAYERS) * OWNED, OWNED)
            piece = rows[tile, pl.ds(first_row, OWNED), :]
            left[p // 2, r, slot, (p % 2) * OWNED:(p % 2 + 1) * OWNED, :] = piece * weight

    pl.semaphore_wait(barrier, len(mates))

    pieces = [(d, q, s, h) for d in ("R", "L") for q in range(CHUNKS) for s in range(SUBS) for h in range(1, HOPS[d, s] + 1)]
    number = {piece: i for i, piece in enumerate(pieces)}

    def tile_of(direction, hops):
        return lax.rem(c + (TILES - 2 * hops if direction == "R" else 2 * hops), TILES)

    def hop_copy(direction, q, s, hop):
        view = right[q].at[tile_of(direction, hop - 1), pl.ds(s * DEPTH, DEPTH)]
        return pltpu.make_async_remote_copy(
            src_ref=view, dst_ref=view, send_sem=ring_send.at[0 if direction == "R" else 1],
            recv_sem=ring_recv.at[number[direction, q, s, hop]], device_id=ring[direction], device_id_type=MESH)

    def take(direction, q, s, hop):
        view = right[q].at[tile_of(direction, hop), pl.ds(s * DEPTH, DEPTH)]
        pltpu.make_async_copy(view, view, ring_recv.at[number[direction, q, s, hop]]).wait()
        pltpu.make_async_remote_copy(
            src_ref=view, dst_ref=view, send_sem=pair_send.at[q], recv_sem=pair_recv.at[q],
            device_id=sibling, device_id_type=MESH).start()

    have_left, have_right = set(), set()
    for step in build_events():
        if step[0] == "send":
            _, direction, q, s, hop = step
            if hop > 1:
                take(direction, q, s, hop - 1)
            hop_copy(direction, q, s, hop).start()
        elif step[0] == "land":
            take(*step[1:])
        elif step[0] == "share":
            view = right[step[1]].at[c]
            pltpu.make_async_remote_copy(
                src_ref=view, dst_ref=view, send_sem=pair_send.at[step[1]], recv_sem=pair_recv.at[step[1]],
                device_id=sibling, device_id_type=MESH).start()
        elif step[0] == "left":
            view = left.at[step[1], r]
            for mate in row_mates:
                pltpu.make_async_remote_copy(
                    src_ref=view, dst_ref=view, send_sem=left_send.at[step[1]], recv_sem=left_recv.at[step[1]],
                    device_id=mate, device_id_type=MESH).start()
        else:
            _, q, h = step
            if q not in have_right:
                have_right.add(q)
                view = right[q].at[pl.ds(0, TILES // 2)]
                pltpu.make_async_copy(view, view, pair_recv.at[q]).wait()
            if h not in have_left:
                have_left.add(h)
                view = left.at[h, pl.ds(0, RUNS - 1)]
                pltpu.make_async_copy(view, view, left_recv.at[h]).wait()
            total = None
            for g in range(RUNS):
                for slot in range(SLOTS):
                    term = jnp.dot(left[h, g, slot], right[q][picks[g][slot]], preferred_element_type=jnp.float32)
                    total = term if total is None else total + term
            partial[q, h] = total
            for p in (2 * h, 2 * h + 1):
                if OFFSETS[p] != 0:
                    pltpu.make_async_remote_copy(
                        src_ref=partial.at[q, h, pl.ds((p % 2) * OWNED, OWNED)], dst_ref=landed.at[q, p],
                        send_sem=sum_send.at[q], recv_sem=sum_recv.at[q],
                        device_id=layer_mates[p], device_id_type=MESH).start()

    def drain(view, sem):
        pltpu.make_async_copy(view, view, sem).wait()

    for i in range(2):
        drain(right[0].at[pl.ds(0, TILES - 2)], ring_send.at[i])
    for h in range(STAGES):
        drain(left.at[h, pl.ds(0, RUNS - 1)], left_send.at[h])
    for q in range(CHUNKS):
        drain(right[q].at[pl.ds(0, TILES // 2)], pair_send.at[q])
    for q in range(CHUNKS):
        drain(landed.at[q], sum_recv.at[q])
        total = partial[q, STAGES - 1, OWNED:, :]
        for p in range(LAYERS - 1):
            total = total + landed[q, p]
        out_ref[:, q * LANES:(q + 1) * LANES] = total
    for q in range(CHUNKS):
        drain(landed.at[q], sum_send.at[q])


def body(iterate_rows, square_slab, row_pattern, slab_pattern, fill_counts, iterate_slab):
    anywhere = pl.BlockSpec(memory_space=pl.ANY)
    dma = pltpu.SemaphoreType.DMA
    product = pl.pallas_call(
        kernel,
        out_shape=jax.ShapeDtypeStruct((OWNED, TILE), jnp.float32),
        in_specs=[anywhere] * 5,
        out_specs=pl.BlockSpec(memory_space=pltpu.VMEM),
        scratch_shapes=[
            pltpu.VMEM((PER_RUN, TILE, TILE), jnp.bfloat16),
            pltpu.VMEM((TILE, TILE), jnp.bfloat16),
            pltpu.SMEM((1, 1, TILES), jnp.int32),
            pltpu.SMEM((1, 1, 1), jnp.int32),
            pltpu.SMEM((1, 1), jnp.int32),
            pltpu.VMEM((STAGES, RUNS, SLOTS, STAGE_ROWS, TILE), jnp.bfloat16),
        ] + [pltpu.VMEM((TILES, TILE, LANES), jnp.bfloat16)] * CHUNKS + [
            pltpu.VMEM((CHUNKS, STAGES, STAGE_ROWS, LANES), jnp.float32),
            pltpu.VMEM((CHUNKS, LAYERS - 1, OWNED, LANES), jnp.float32),
            dma((PER_RUN + 1,)), dma((3,)),
            dma((STAGES,)), dma((STAGES,)),
            dma((2,)), dma((CHUNKS * SUBS * (CHIPS - 1),)),
            dma((CHUNKS,)), dma((CHUNKS,)),
            dma((CHUNKS,)), dma((CHUNKS,)),
        ],
        compiler_params=pltpu.CompilerParams(
            collective_id=0, has_side_effects=True, vmem_limit_bytes=40 << 20),
        name="sparse_product",
    )(iterate_rows, square_slab, row_pattern, slab_pattern, fill_counts)
    return 1.5 * iterate_slab - 0.5 * product


def solution(mesh):
    return jax.shard_map(
        body,
        mesh=mesh,
        in_specs=(
            P("layer", "col", "row"),
            P("layer", "col", "row"),
            P("layer", "col", None),
            P("layer", "col", "row"),
            P("layer", "col"),
            P(("col", "layer"), "row"),
        ),
        out_specs=P(("col", "layer"), "row"),
        check_vma=False,
    )
```

```python
import functools

import jax
import jax.numpy as jnp
from jax import lax
from jax.experimental import pallas as pl
from jax.experimental.pallas import tpu as pltpu
from jax.sharding import PartitionSpec as P

MESH = pl.DeviceIdType.MESH
TILE = 512
RUNS = 4
PER_RUN = 4
SLOTS = 2
TILES = 16
CHIPS = 8
LAYERS = 8
LANES = 128
PARTS = (128, 128, 64, 64, 64, 64)
STARTS = tuple(sum(PARTS[:p]) for p in range(len(PARTS)))
DEPTH = TILE // 2
PIECES = tuple((p, s) for p, width in enumerate(PARTS) for s in range(width // 64))
STAGES = 4
OWNED = TILE // LAYERS
STAGE_ROWS = TILE // STAGES
OFFSETS = (4, 3, 5, 2, 6, 1, 7, 0)
HOPS = {
    "R": {u: 4 - i % 2 for i, u in enumerate(PIECES)},
    "L": {u: 3 + i % 2 for i, u in enumerate(PIECES)},
}

SLOT = 1.4
LATENCY = 2.7
DEADLINES = (21, 23, 25, 33, 35, 38)
SEND_LEFT = (0.0, 0.0, 8.3, 13.8)
PASS_LEFT = (8.2, 13.7, 22.0, 30.2)
HAVE_LEFT = (20.0, 28.5, 37.0, 40.0)


def ring_order(direction):
    hops = HOPS[direction]
    done = dict.fromkeys(hops, 0)
    ready = dict.fromkeys(hops, 0.0)
    order, now = [], 0.0
    while done != hops:
        left = [u for u in PIECES if done[u] < hops[u]]
        now = max(now, min(ready[u] for u in left))
        active = [u for u in left if ready[u] <= now]
        u = min(active, key=lambda u: (DEADLINES[u[0]] - (SLOT + LATENCY) * (hops[u] - done[u] - 1), u))
        done[u] += 1
        order.append((now, u, done[u]))
        now += SLOT
        ready[u] = now + LATENCY
    return order


def build_events():
    events = []
    complete = [0.0] * len(PARTS)
    for direction in ("R", "L"):
        arrived = {}
        for now, u, hop in ring_order(direction):
            events.append((max(now - SLOT, arrived.get(u, 0.0)), 1, now, ("send", direction, u, hop)))
            arrived[u] = now + SLOT + LATENCY
        for u, when in arrived.items():
            events.append((when, 0, when, ("land", direction, u, HOPS[direction][u])))
            complete[u[0]] = max(complete[u[0]], when)
    for p in range(len(PARTS)):
        events.append((1.5 * STARTS[p] / 64, 2, p, ("share", p)))
        for h in range(STAGES):
            events.append((max(complete[p] + 1.0, HAVE_LEFT[h]), 4, h, ("block", p, h)))
    for h in range(STAGES):
        events.append((SEND_LEFT[h], 3, h, ("left", h)))
        events.append((PASS_LEFT[h], 3, h, ("pass", h)))
    return [e[3] for e in sorted(events, key=lambda e: e[:3])]


def kernel(
    rows_hbm, slab_hbm, pattern_hbm, kept_hbm, fill_hbm, out_ref,
    rows, slab, pattern, kept, fill, left, in_sem, scalar_sem, left_send, left_recv,
    ring_send, ring_recv, pair_send, pair_recv, sum_send, sum_recv, *buffers,
):
    count_parts = len(PARTS)
    right, partial, landed = (buffers[i * count_parts:(i + 1) * count_parts] for i in range(3))
    r, c, l = (lax.axis_index(name) for name in ("row", "col", "layer"))
    core = lax.rem(c, 2)
    sibling = (r, c + 1 - 2 * core, l)
    ring = {"R": (r, lax.rem(c + 2, TILES), l), "L": (r, lax.rem(c + TILES - 2, TILES), l)}
    row_ring = [(lax.rem(r + o, RUNS), c, l) for o in (1, RUNS - 1)]
    row_from = [lax.rem(r + o, RUNS) for o in (RUNS - 1, 1)]
    layer_mates = [(r, c, lax.rem(l + o, LAYERS)) for o in OFFSETS[:-1]]

    slab_copy = pltpu.make_async_copy(slab_hbm.at[0], slab, in_sem.at[PER_RUN])
    scalar_copies = [
        pltpu.make_async_copy(pattern_hbm, pattern, scalar_sem.at[0]),
        pltpu.make_async_copy(kept_hbm, kept, scalar_sem.at[1]),
        pltpu.make_async_copy(fill_hbm, fill, scalar_sem.at[2]),
    ]
    tile_copies = [
        pltpu.make_async_copy(rows_hbm.at[0, :, pl.ds(t * TILE, TILE)], rows.at[t], in_sem.at[t])
        for t in range(PER_RUN)
    ]
    for copy in scalar_copies + [slab_copy] + tile_copies:
        copy.start()

    barrier = pltpu.get_barrier_semaphore()
    mates = layer_mates + row_ring + [ring["R"], ring["L"], sibling]
    for mate in mates:
        pl.semaphore_signal(barrier, inc=1, device_id=mate, device_id_type=MESH)

    for copy in scalar_copies:
        copy.wait()
    picks = []
    for g in range(RUNS):
        bits = [pattern[0, 0, g * PER_RUN + t] > 0 for t in range(PER_RUN)]
        first = jnp.where(bits[0], 0, jnp.where(bits[1], 1, jnp.where(bits[2], 2, 3)))
        final = jnp.where(bits[3], 3, jnp.where(bits[2], 2, jnp.where(bits[1], 1, 0)))
        picks.append((g * PER_RUN + first, g * PER_RUN + final))
    own = [pattern[0, 0, r * PER_RUN + t] for t in range(PER_RUN)]
    count = own[0] + own[1] + own[2] + own[3]
    own_first = jnp.where(own[0] > 0, 0, jnp.where(own[1] > 0, 1, jnp.where(own[2] > 0, 2, 3)))
    own_final = jnp.where(own[3] > 0, 3, jnp.where(own[2] > 0, 2, jnp.where(own[1] > 0, 1, 0)))

    slab_copy.wait()
    limit = jnp.where(kept[0, 0, 0] > 0, fill[0, 0], 0)
    live = lax.broadcasted_iota(jnp.int32, (TILE, LANES), 0) < limit
    low = lax.broadcasted_iota(jnp.int32, (DEPTH, LANES), 1) < 64

    def swap(x):
        return pltpu.roll(x, 64, 1)

    for p, width in enumerate(PARTS):
        base = STARTS[p] // LANES * LANES
        piece = jnp.where(live, slab[:, base:base + LANES].astype(jnp.float32), 0.0)
        if width == 64:
            top, bottom = piece[:DEPTH], piece[DEPTH:]
            piece = jnp.where(low, top, swap(bottom)) if STARTS[p] == base else jnp.where(low, swap(top), bottom)
        right[p][c] = piece.astype(jnp.bfloat16)

    pl.semaphore_wait(barrier, len(mates))

    hop_list = [(d, u, h) for d in ("R", "L") for u in PIECES for h in range(1, HOPS[d][u] + 1)]
    number = {piece: i for i, piece in enumerate(hop_list)}

    def piece_view(direction, u, hops):
        tile = lax.rem(c + (TILES - 2 * hops if direction == "R" else 2 * hops), TILES)
        return right[u[0]].at[tile, pl.ds(u[1] * DEPTH, DEPTH)]

    def to_sibling(p, view):
        pltpu.make_async_remote_copy(
            src_ref=view, dst_ref=view, send_sem=pair_send.at[p], recv_sem=pair_recv.at[p],
            device_id=sibling, device_id_type=MESH).start()

    def hop_copy(direction, u, hop):
        view = piece_view(direction, u, hop - 1)
        return pltpu.make_async_remote_copy(
            src_ref=view, dst_ref=view, send_sem=ring_send.at[0 if direction == "R" else 1],
            recv_sem=ring_recv.at[number[direction, u, hop]], device_id=ring[direction], device_id_type=MESH)

    def arrive(direction, u, hop):
        view = piece_view(direction, u, hop)
        pltpu.make_async_copy(view, view, ring_recv.at[number[direction, u, hop]]).wait()
        return view

    def fill_stage(h):
        for slot, (tile, least) in enumerate(((own_first, 1), (own_final, 2))):
            weight = jnp.full((OWNED, TILE), jnp.where(count >= least, 1.0, 0.0), jnp.float32).astype(jnp.bfloat16)
            for half in range(2):
                first_row = pl.multiple_of(lax.rem(l + OFFSETS[2 * h + half], LAYERS) * OWNED, OWNED)
                piece = rows[tile, pl.ds(first_row, OWNED), :]
                left[h, r, slot, half * OWNED:(half + 1) * OWNED, :] = piece * weight

    def left_copy(h, way):
        view = left.at[h, r]
        return pltpu.make_async_remote_copy(
            src_ref=view, dst_ref=view, send_sem=left_send.at[h], recv_sem=left_recv.at[h, way],
            device_id=row_ring[way], device_id_type=MESH)

    def pass_copy(h, way):
        view = left.at[h, row_from[way], way]
        return pltpu.make_async_remote_copy(
            src_ref=view, dst_ref=view, send_sem=left_send.at[h], recv_sem=left_recv.at[h, 2],
            device_id=row_ring[way], device_id_type=MESH)

    have_rows, have_left, have_right = False, set(), set()
    for step in build_events():
        if step[0] == "send":
            _, direction, u, hop = step
            view = arrive(direction, u, hop - 1) if hop > 1 else None
            hop_copy(direction, u, hop).start()
            if view is not None:
                to_sibling(u[0], view)
        elif step[0] == "land":
            to_sibling(step[2][0], arrive(*step[1:]))
        elif step[0] == "share":
            to_sibling(step[1], right[step[1]].at[c])
        elif step[0] == "left":
            if not have_rows:
                have_rows = True
                for copy in tile_copies:
                    copy.wait()
            fill_stage(step[1])
            for way in range(2):
                left_copy(step[1], way).start()
        elif step[0] == "pass":
            for way in range(2):
                view = left.at[step[1], row_from[way]]
                pltpu.make_async_copy(view, view, left_recv.at[step[1], way]).wait()
                pass_copy(step[1], way).start()
        else:
            _, p, h = step
            if p not in have_right:
                have_right.add(p)
                view = right[p].at[pl.ds(0, TILES // 2)]
                pltpu.make_async_copy(view, view, pair_recv.at[p]).wait()
            if h not in have_left:
                have_left.add(h)
                view = left.at[h, 0]
                pltpu.make_async_copy(view, view, left_recv.at[h, 2]).wait()
            totals = [None, None]
            for g in range(RUNS):
                for slot in range(SLOTS):
                    tile = right[p][picks[g][slot]]
                    if PARTS[p] == LANES:
                        terms = [jnp.dot(left[h, g, slot], tile, preferred_element_type=jnp.float32)]
                    else:
                        terms = [
                            jnp.dot(left[h, g, slot, :, :DEPTH], tile, preferred_element_type=jnp.float32),
                            jnp.dot(left[h, g, slot, :, DEPTH:], tile, preferred_element_type=jnp.float32),
                        ]
                    for i, term in enumerate(terms):
                        totals[i] = term if totals[i] is None else totals[i] + term
            if PARTS[p] == LANES:
                partial[p][h] = totals[0].reshape(2, OWNED, LANES)
            else:
                in_low = totals[0] + swap(totals[1])
                in_high = swap(totals[0]) + totals[1]
                for half in range(2):
                    row = half * OWNED
                    partial[p][h, half] = jnp.where(
                        low[:OWNED // 2], in_low[row:row + OWNED // 2], in_high[row + OWNED // 2:row + OWNED])
            for half in range(2):
                k = 2 * h + half
                if OFFSETS[k] != 0:
                    pltpu.make_async_remote_copy(
                        src_ref=partial[p].at[h, half], dst_ref=landed[p].at[k],
                        send_sem=sum_send.at[p], recv_sem=sum_recv.at[p],
                        device_id=layer_mates[k], device_id_type=MESH).start()

    def drain(view, sem):
        pltpu.make_async_copy(view, view, sem).wait()

    for i in range(2):
        drain(right[0].at[pl.ds(0, TILES - 2)], ring_send.at[i])
    for h in range(STAGES):
        drain(left.at[h, pl.ds(0, RUNS - 1)], left_send.at[h])
    for p in range(count_parts):
        drain(right[p].at[pl.ds(0, TILES // 2)], pair_send.at[p])
    sums = []
    for p in range(count_parts):
        drain(landed[p], sum_recv.at[p])
        total = partial[p][STAGES - 1, 1]
        for k in range(LAYERS - 1):
            total = total + landed[p][k]
        sums.append(total)
        base = STARTS[p] // LANES * LANES
        if PARTS[p] == LANES:
            out_ref[:, base:base + LANES] = total
        elif STARTS[p] > base:
            one, two = sums[p - 1], sums[p]
            out_ref[:OWNED // 2, base:base + LANES] = jnp.where(low[:OWNED // 2], one, swap(two))
            out_ref[OWNED // 2:, base:base + LANES] = jnp.where(low[:OWNED // 2], swap(one), two)
    for p in range(count_parts):
        drain(landed[p], sum_send.at[p])


def body(iterate_rows, square_slab, row_pattern, slab_pattern, fill_counts, iterate_slab):
    in_hbm = pl.BlockSpec(memory_space=pltpu.HBM)
    dma = pltpu.SemaphoreType.DMA
    parts = len(PARTS)
    deep = [width // 64 for width in PARTS]
    product = pl.pallas_call(
        kernel,
        out_shape=jax.ShapeDtypeStruct((OWNED, TILE), jnp.float32),
        in_specs=[in_hbm] * 5,
        out_specs=pl.BlockSpec(memory_space=pltpu.VMEM),
        scratch_shapes=[
            pltpu.VMEM((PER_RUN, TILE, TILE), jnp.bfloat16),
            pltpu.VMEM((TILE, TILE), jnp.bfloat16),
            pltpu.SMEM((1, 1, TILES), jnp.int32),
            pltpu.SMEM((1, 1, 1), jnp.int32),
            pltpu.SMEM((1, 1), jnp.int32),
            pltpu.VMEM((STAGES, RUNS, SLOTS, STAGE_ROWS, TILE), jnp.bfloat16),
            dma((PER_RUN + 1,)), dma((3,)),
            dma((STAGES,)), dma((STAGES, 3)),
            dma((2,)), dma((len(PIECES) * (CHIPS - 1),)),
            dma((parts,)), dma((parts,)), dma((parts,)), dma((parts,)),
        ]
        + [pltpu.VMEM((TILES, d * DEPTH, LANES), jnp.bfloat16) for d in deep]
        + [pltpu.VMEM((STAGES, 2, d * OWNED // 2, LANES), jnp.float32) for d in deep]
        + [pltpu.VMEM((LAYERS - 1, d * OWNED // 2, LANES), jnp.float32) for d in deep],
        compiler_params=pltpu.CompilerParams(
            collective_id=0, has_side_effects=True, vmem_limit_bytes=60 << 20),
        name="sparse_product",
    )(iterate_rows, square_slab, row_pattern, slab_pattern, fill_counts)
    return 1.5 * iterate_slab - 0.5 * product


def solution(mesh):
    return jax.shard_map(
        body,
        mesh=mesh,
        in_specs=(
            P("layer", "col", "row"),
            P("layer", "col", "row"),
            P("layer", "col", None),
            P("layer", "col", "row"),
            P("layer", "col"),
            P(("col", "layer"), "row"),
        ),
        out_specs=P(("col", "layer"), "row"),
        check_vma=False,
    )
```

```python
import functools

import jax
import jax.numpy as jnp
from jax import lax
from jax.experimental import pallas as pl
from jax.experimental.pallas import tpu as pltpu
from jax.sharding import PartitionSpec as P

MESH = pl.DeviceIdType.MESH
TILE = 512
RUNS = 4
PER_RUN = 4
SLOTS = 2
TILES = 16
CHIPS = 8
LAYERS = 8
LANES = 128
PARTS = (128, 128, 64, 64, 64, 64)
STARTS = tuple(sum(PARTS[:p]) for p in range(len(PARTS)))
DEPTH = TILE // 2
PIECES = tuple((p, s) for p, width in enumerate(PARTS) for s in range(width // 64))
STAGES = 4
OWNED = TILE // LAYERS
STAGE_ROWS = TILE // STAGES
OFFSETS = (4, 3, 5, 2, 6, 1, 7, 0)
HOPS = {
    "R": {u: 4 - i % 2 for i, u in enumerate(PIECES)},
    "L": {u: 3 + i % 2 for i, u in enumerate(PIECES)},
}

SLOT = 1.4
LATENCY = 2.7
DEADLINES = (21, 23, 25, 33, 35, 38)
SEND_LEFT = (0.0, 0.0, 8.3, 13.8)
PASS_LEFT = (8.2, 13.7, 22.0, 30.2)
HAVE_LEFT = (20.0, 28.5, 37.0, 40.0)
GREET = (10.0, 14.0, 17.0, 19.0)


def ring_order(direction):
    hops = HOPS[direction]
    done = dict.fromkeys(hops, 0)
    ready = dict.fromkeys(hops, 0.0)
    order, now = [], 0.0
    while done != hops:
        left = [u for u in PIECES if done[u] < hops[u]]
        now = max(now, min(ready[u] for u in left))
        active = [u for u in left if ready[u] <= now]
        u = min(active, key=lambda u: (DEADLINES[u[0]] - (SLOT + LATENCY) * (hops[u] - done[u] - 1), u))
        done[u] += 1
        order.append((now, u, done[u]))
        now += SLOT
        ready[u] = now + LATENCY
    return order


def build_events():
    events = []
    complete = [0.0] * len(PARTS)
    for direction in ("R", "L"):
        arrived = {}
        for now, u, hop in ring_order(direction):
            events.append((max(now - SLOT, arrived.get(u, 0.0)), 1, now, ("send", direction, u, hop)))
            arrived[u] = now + SLOT + LATENCY
        for u, when in arrived.items():
            events.append((when, 0, when, ("land", direction, u, HOPS[direction][u])))
            complete[u[0]] = max(complete[u[0]], when)
    for p in range(len(PARTS)):
        events.append((1.5 * STARTS[p] / 64, 2, p, ("share", p)))
        for h in range(STAGES):
            events.append((max(complete[p] + 1.0, HAVE_LEFT[h]), 4, h, ("block", p, h)))
    for h in range(STAGES):
        events.append((SEND_LEFT[h], 3, h, ("left", h)))
        events.append((PASS_LEFT[h], 3, h, ("pass", h)))
    for k in range(len(GREET)):
        events.append((GREET[k], 3, k, ("greet", k)))
    return [e[3] for e in sorted(events, key=lambda e: e[:3])]


def kernel(
    rows_hbm, slab_hbm, pattern_hbm, kept_hbm, fill_hbm, iterate_hbm, out_ref,
    rows, slab, pattern, kept, fill, iterate, left, in_sem, scalar_sem, left_send, left_recv,
    ring_send, ring_recv, pair_send, pair_recv, sum_send, sum_recv, greet_sem, *buffers,
):
    count_parts = len(PARTS)
    right, partial, landed = (buffers[i * count_parts:(i + 1) * count_parts] for i in range(3))
    r, c, l = (lax.axis_index(name) for name in ("row", "col", "layer"))
    core = lax.rem(c, 2)
    sibling = (r, c + 1 - 2 * core, l)
    ring = {"R": (r, lax.rem(c + 2, TILES), l), "L": (r, lax.rem(c + TILES - 2, TILES), l)}
    row_ring = [(lax.rem(r + o, RUNS), c, l) for o in (1, RUNS - 1)]
    row_from = [lax.rem(r + o, RUNS) for o in (RUNS - 1, 1)]
    layer_mates = [(r, c, lax.rem(l + o, LAYERS)) for o in OFFSETS[:-1]]

    slab_copy = pltpu.make_async_copy(slab_hbm.at[0], slab, in_sem.at[PER_RUN])
    scalar_copies = [
        pltpu.make_async_copy(pattern_hbm, pattern, scalar_sem.at[0]),
        pltpu.make_async_copy(kept_hbm, kept, scalar_sem.at[1]),
        pltpu.make_async_copy(fill_hbm, fill, scalar_sem.at[2]),
    ]
    tile_copies = [
        pltpu.make_async_copy(rows_hbm.at[0, :, pl.ds(t * TILE, TILE)], rows.at[t], in_sem.at[t])
        for t in range(PER_RUN)
    ]
    iterate_copy = pltpu.make_async_copy(iterate_hbm, iterate, in_sem.at[PER_RUN + 1])
    for copy in scalar_copies + [slab_copy] + tile_copies + [iterate_copy]:
        copy.start()

    barrier = pltpu.get_barrier_semaphore()
    above, below = (r, c, lax.rem(l + 1, LAYERS)), (r, c, lax.rem(l + LAYERS - 1, LAYERS))
    mates = row_ring + [ring["R"], ring["L"], sibling]
    for mate in mates + [below]:
        pl.semaphore_signal(barrier, inc=1, device_id=mate, device_id_type=MESH)

    for copy in scalar_copies:
        copy.wait()
    picks = []
    for g in range(RUNS):
        bits = [pattern[0, 0, g * PER_RUN + t] > 0 for t in range(PER_RUN)]
        first = jnp.where(bits[0], 0, jnp.where(bits[1], 1, jnp.where(bits[2], 2, 3)))
        final = jnp.where(bits[3], 3, jnp.where(bits[2], 2, jnp.where(bits[1], 1, 0)))
        picks.append((g * PER_RUN + first, g * PER_RUN + final))
    own = [pattern[0, 0, r * PER_RUN + t] for t in range(PER_RUN)]
    count = own[0] + own[1] + own[2] + own[3]
    own_first = jnp.where(own[0] > 0, 0, jnp.where(own[1] > 0, 1, jnp.where(own[2] > 0, 2, 3)))
    own_final = jnp.where(own[3] > 0, 3, jnp.where(own[2] > 0, 2, jnp.where(own[1] > 0, 1, 0)))

    slab_copy.wait()
    limit = jnp.where(kept[0, 0, 0] > 0, fill[0, 0], 0)
    live = lax.broadcasted_iota(jnp.int32, (TILE, LANES), 0) < limit
    low = lax.broadcasted_iota(jnp.int32, (DEPTH, LANES), 1) < 64

    def swap(x):
        return pltpu.roll(x, 64, 1)

    for p, width in enumerate(PARTS):
        base = STARTS[p] // LANES * LANES
        piece = jnp.where(live, slab[:, base:base + LANES].astype(jnp.float32), 0.0)
        if width == 64:
            top, bottom = piece[:DEPTH], piece[DEPTH:]
            piece = jnp.where(low, top, swap(bottom)) if STARTS[p] == base else jnp.where(low, swap(top), bottom)
        right[p][c] = piece.astype(jnp.bfloat16)

    pl.semaphore_wait(barrier, len(mates) + 1)
    pl.semaphore_signal(greet_sem.at[0], inc=1, device_id=above, device_id_type=MESH)

    hop_list = [(d, u, h) for d in ("R", "L") for u in PIECES for h in range(1, HOPS[d][u] + 1)]
    number = {piece: i for i, piece in enumerate(hop_list)}

    def piece_view(direction, u, hops):
        tile = lax.rem(c + (TILES - 2 * hops if direction == "R" else 2 * hops), TILES)
        return right[u[0]].at[tile, pl.ds(u[1] * DEPTH, DEPTH)]

    def to_sibling(p, view):
        pltpu.make_async_remote_copy(
            src_ref=view, dst_ref=view, send_sem=pair_send.at[p], recv_sem=pair_recv.at[p],
            device_id=sibling, device_id_type=MESH).start()

    def hop_copy(direction, u, hop):
        view = piece_view(direction, u, hop - 1)
        return pltpu.make_async_remote_copy(
            src_ref=view, dst_ref=view, send_sem=ring_send.at[0 if direction == "R" else 1],
            recv_sem=ring_recv.at[number[direction, u, hop]], device_id=ring[direction], device_id_type=MESH)

    def arrive(direction, u, hop):
        view = piece_view(direction, u, hop)
        pltpu.make_async_copy(view, view, ring_recv.at[number[direction, u, hop]]).wait()
        return view

    def fill_stage(h):
        for slot, (tile, least) in enumerate(((own_first, 1), (own_final, 2))):
            weight = jnp.full((OWNED, TILE), jnp.where(count >= least, 1.0, 0.0), jnp.float32).astype(jnp.bfloat16)
            for half in range(2):
                first_row = pl.multiple_of(lax.rem(l + OFFSETS[2 * h + half], LAYERS) * OWNED, OWNED)
                piece = rows[tile, pl.ds(first_row, OWNED), :]
                left[h, r, slot, half * OWNED:(half + 1) * OWNED, :] = piece * weight

    def left_copy(h, way):
        view = left.at[h, r]
        return pltpu.make_async_remote_copy(
            src_ref=view, dst_ref=view, send_sem=left_send.at[h], recv_sem=left_recv.at[h, way],
            device_id=row_ring[way], device_id_type=MESH)

    def pass_copy(h, way):
        view = left.at[h, row_from[way], way]
        return pltpu.make_async_remote_copy(
            src_ref=view, dst_ref=view, send_sem=left_send.at[h], recv_sem=left_recv.at[h, 2],
            device_id=row_ring[way], device_id_type=MESH)

    have_rows, have_left, have_right = False, set(), set()
    for step in build_events():
        if step[0] == "send":
            _, direction, u, hop = step
            view = arrive(direction, u, hop - 1) if hop > 1 else None
            hop_copy(direction, u, hop).start()
            if view is not None:
                to_sibling(u[0], view)
        elif step[0] == "land":
            to_sibling(step[2][0], arrive(*step[1:]))
        elif step[0] == "greet":
            k = step[1]
            pl.semaphore_wait(greet_sem.at[k], 1 if k == 0 else 2)
            if k + 1 < len(GREET):
                for mate in (above, below):
                    pl.semaphore_signal(greet_sem.at[k + 1], inc=1, device_id=mate, device_id_type=MESH)
        elif step[0] == "share":
            to_sibling(step[1], right[step[1]].at[c])
        elif step[0] == "left":
            if not have_rows:
                have_rows = True
                for copy in tile_copies:
                    copy.wait()
            fill_stage(step[1])
            for way in range(2):
                left_copy(step[1], way).start()
        elif step[0] == "pass":
            for way in range(2):
                view = left.at[step[1], row_from[way]]
                pltpu.make_async_copy(view, view, left_recv.at[step[1], way]).wait()
                pass_copy(step[1], way).start()
        else:
            _, p, h = step
            if p not in have_right:
                have_right.add(p)
                view = right[p].at[pl.ds(0, TILES // 2)]
                pltpu.make_async_copy(view, view, pair_recv.at[p]).wait()
            if h not in have_left:
                have_left.add(h)
                view = left.at[h, 0]
                pltpu.make_async_copy(view, view, left_recv.at[h, 2]).wait()
            totals = [None, None]
            for g in range(RUNS):
                for slot in range(SLOTS):
                    tile = right[p][picks[g][slot]]
                    if PARTS[p] == LANES:
                        terms = [jnp.dot(left[h, g, slot], tile, preferred_element_type=jnp.float32)]
                    else:
                        terms = [
                            jnp.dot(left[h, g, slot, :, :DEPTH], tile, preferred_element_type=jnp.float32),
                            jnp.dot(left[h, g, slot, :, DEPTH:], tile, preferred_element_type=jnp.float32),
                        ]
                    for i, term in enumerate(terms):
                        totals[i] = term if totals[i] is None else totals[i] + term
            if PARTS[p] == LANES:
                partial[p][h] = totals[0].reshape(2, OWNED, LANES)
            else:
                in_low = totals[0] + swap(totals[1])
                in_high = swap(totals[0]) + totals[1]
                for half in range(2):
                    row = half * OWNED
                    partial[p][h, half] = jnp.where(
                        low[:OWNED // 2], in_low[row:row + OWNED // 2], in_high[row + OWNED // 2:row + OWNED])
            for half in range(2):
                k = 2 * h + half
                if OFFSETS[k] != 0:
                    pltpu.make_async_remote_copy(
                        src_ref=partial[p].at[h, half], dst_ref=landed[p].at[k],
                        send_sem=sum_send.at[p], recv_sem=sum_recv.at[p],
                        device_id=layer_mates[k], device_id_type=MESH).start()

    def drain(view, sem):
        pltpu.make_async_copy(view, view, sem).wait()

    for i in range(2):
        drain(right[0].at[pl.ds(0, TILES - 2)], ring_send.at[i])
    for h in range(STAGES):
        drain(left.at[h, pl.ds(0, RUNS - 1)], left_send.at[h])
    for p in range(count_parts):
        drain(right[p].at[pl.ds(0, TILES // 2)], pair_send.at[p])
    iterate_copy.wait()
    sums = []

    def finish(first_row, last_row, base, total):
        out_ref[first_row:last_row, base:base + LANES] = (
            1.5 * iterate[first_row:last_row, base:base + LANES] - 0.5 * total)

    for p in range(count_parts):
        drain(landed[p], sum_recv.at[p])
        total = partial[p][STAGES - 1, 1]
        for k in range(LAYERS - 1):
            total = total + landed[p][k]
        sums.append(total)
        base = STARTS[p] // LANES * LANES
        if PARTS[p] == LANES:
            finish(0, OWNED, base, total)
        elif STARTS[p] > base:
            one, two = sums[p - 1], sums[p]
            finish(0, OWNED // 2, base, jnp.where(low[:OWNED // 2], one, swap(two)))
            finish(OWNED // 2, OWNED, base, jnp.where(low[:OWNED // 2], swap(one), two))
    for p in range(count_parts):
        drain(landed[p], sum_send.at[p])


def body(iterate_rows, square_slab, row_pattern, slab_pattern, fill_counts, iterate_slab):
    in_hbm = pl.BlockSpec(memory_space=pltpu.HBM)
    dma = pltpu.SemaphoreType.DMA
    parts = len(PARTS)
    deep = [width // 64 for width in PARTS]
    return pl.pallas_call(
        kernel,
        out_shape=jax.ShapeDtypeStruct((OWNED, TILE), jnp.float32),
        in_specs=[in_hbm] * 6,
        out_specs=pl.BlockSpec(memory_space=pltpu.VMEM),
        scratch_shapes=[
            pltpu.VMEM((PER_RUN, TILE, TILE), jnp.bfloat16),
            pltpu.VMEM((TILE, TILE), jnp.bfloat16),
            pltpu.SMEM((1, 1, TILES), jnp.int32),
            pltpu.SMEM((1, 1, 1), jnp.int32),
            pltpu.SMEM((1, 1), jnp.int32),
            pltpu.VMEM((OWNED, TILE), jnp.float32),
            pltpu.VMEM((STAGES, RUNS, SLOTS, STAGE_ROWS, TILE), jnp.bfloat16),
            dma((PER_RUN + 2,)), dma((3,)),
            dma((STAGES,)), dma((STAGES, 3)),
            dma((2,)), dma((len(PIECES) * (CHIPS - 1),)),
            dma((parts,)), dma((parts,)), dma((parts,)), dma((parts,)),
            pltpu.SemaphoreType.REGULAR((len(GREET),)),
        ]
        + [pltpu.VMEM((TILES, d * DEPTH, LANES), jnp.bfloat16) for d in deep]
        + [pltpu.VMEM((STAGES, 2, d * OWNED // 2, LANES), jnp.float32) for d in deep]
        + [pltpu.VMEM((LAYERS - 1, d * OWNED // 2, LANES), jnp.float32) for d in deep],
        compiler_params=pltpu.CompilerParams(
            collective_id=0, has_side_effects=True, vmem_limit_bytes=60 << 20),
        name="sparse_product",
    )(iterate_rows, square_slab, row_pattern, slab_pattern, fill_counts, iterate_slab)


def solution(mesh):
    return jax.shard_map(
        body,
        mesh=mesh,
        in_specs=(
            P("layer", "col", "row"),
            P("layer", "col", "row"),
            P("layer", "col", None),
            P("layer", "col", "row"),
            P("layer", "col"),
            P(("col", "layer"), "row"),
        ),
        out_specs=P(("col", "layer"), "row"),
        check_vma=False,
    )
```

```python
import functools

import jax
import jax.numpy as jnp
from jax import lax
from jax.experimental import pallas as pl
from jax.experimental.pallas import tpu as pltpu
from jax.sharding import PartitionSpec as P

MESH = pl.DeviceIdType.MESH
TILE = 512
RUNS = 4
PER_RUN = 4
SLOTS = 2
TILES = 16
CHIPS = 8
LAYERS = 8
LANES = 128
PARTS = (128, 128, 64, 64, 64, 64)
STARTS = tuple(sum(PARTS[:p]) for p in range(len(PARTS)))
DEPTH = TILE // 2
PIECES = tuple((p, s) for p, width in enumerate(PARTS) for s in range(width // 64))
STAGES = 4
OWNED = TILE // LAYERS
STAGE_ROWS = TILE // STAGES
OFFSETS = (4, 3, 5, 2, 6, 1, 7, 0)
HOPS = {
    "R": {u: 4 - i % 2 for i, u in enumerate(PIECES)},
    "L": {u: 3 + i % 2 for i, u in enumerate(PIECES)},
}

SLOT = 1.4
LATENCY = 2.7
DEADLINES = (21, 23, 25, 33, 35, 38)
SEND_LEFT = (0.0, 0.0, 8.3, 13.8)
PASS_LEFT = (8.2, 13.7, 22.0, 30.2)
HAVE_LEFT = (20.0, 28.5, 37.0, 40.0)
GREET = (10.0, 14.0, 17.0, 19.0)


def ring_order(direction):
    hops = HOPS[direction]
    done = dict.fromkeys(hops, 0)
    ready = dict.fromkeys(hops, 0.0)
    order, now = [], 0.0
    while done != hops:
        left = [u for u in PIECES if done[u] < hops[u]]
        now = max(now, min(ready[u] for u in left))
        active = [u for u in left if ready[u] <= now]
        u = min(active, key=lambda u: (DEADLINES[u[0]] - (SLOT + LATENCY) * (hops[u] - done[u] - 1), u))
        done[u] += 1
        order.append((now, u, done[u]))
        now += SLOT
        ready[u] = now + LATENCY
    return order


def build_events():
    events = []
    complete = [0.0] * len(PARTS)
    for direction in ("R", "L"):
        arrived = {}
        for now, u, hop in ring_order(direction):
            events.append((max(now - SLOT, arrived.get(u, 0.0)), 1, now, ("send", direction, u, hop)))
            arrived[u] = now + SLOT + LATENCY
        for u, when in arrived.items():
            events.append((when, 0, when, ("land", direction, u, HOPS[direction][u])))
            complete[u[0]] = max(complete[u[0]], when)
    for p in range(len(PARTS)):
        events.append((1.5 * STARTS[p] / 64, 2, p, ("share", p)))
        for h in range(STAGES):
            events.append((max(complete[p] + 1.0, HAVE_LEFT[h]), 4, h, ("block", p, h)))
    for h in range(STAGES):
        events.append((SEND_LEFT[h], 3, h, ("left", h)))
        events.append((PASS_LEFT[h], 3, h, ("pass", h)))
    for k in range(len(GREET)):
        events.append((GREET[k], 3, k, ("greet", k)))
    return [e[3] for e in sorted(events, key=lambda e: e[:3])]


def kernel(
    rows_hbm, slab_hbm, pattern_hbm, kept_hbm, fill_hbm, out_ref,
    rows, slab, pattern, kept, fill, left, in_sem, scalar_sem, left_send, left_recv,
    ring_send, ring_recv, pair_send, pair_recv, sum_send, sum_recv, greet_sem, *buffers,
):
    count_parts = len(PARTS)
    right, partial, landed = (buffers[i * count_parts:(i + 1) * count_parts] for i in range(3))
    r, c, l = (lax.axis_index(name) for name in ("row", "col", "layer"))
    core = lax.rem(c, 2)
    sibling = (r, c + 1 - 2 * core, l)
    ring = {"R": (r, lax.rem(c + 2, TILES), l), "L": (r, lax.rem(c + TILES - 2, TILES), l)}
    row_ring = [(lax.rem(r + o, RUNS), c, l) for o in (1, RUNS - 1)]
    row_from = [lax.rem(r + o, RUNS) for o in (RUNS - 1, 1)]
    layer_mates = [(r, c, lax.rem(l + o, LAYERS)) for o in OFFSETS[:-1]]

    slab_copy = pltpu.make_async_copy(slab_hbm.at[0], slab, in_sem.at[PER_RUN])
    scalar_copies = [
        pltpu.make_async_copy(pattern_hbm, pattern, scalar_sem.at[0]),
        pltpu.make_async_copy(kept_hbm, kept, scalar_sem.at[1]),
        pltpu.make_async_copy(fill_hbm, fill, scalar_sem.at[2]),
    ]
    tile_copies = [
        pltpu.make_async_copy(rows_hbm.at[0, :, pl.ds(t * TILE, TILE)], rows.at[t], in_sem.at[t])
        for t in range(PER_RUN)
    ]
    for copy in scalar_copies + [slab_copy] + tile_copies:
        copy.start()

    barrier = pltpu.get_barrier_semaphore()
    above, below = (r, c, lax.rem(l + 1, LAYERS)), (r, c, lax.rem(l + LAYERS - 1, LAYERS))
    mates = row_ring + [ring["R"], ring["L"], sibling]
    for mate in mates + [below]:
        pl.semaphore_signal(barrier, inc=1, device_id=mate, device_id_type=MESH)

    for copy in scalar_copies:
        copy.wait()
    picks = []
    for g in range(RUNS):
        bits = [pattern[0, 0, g * PER_RUN + t] > 0 for t in range(PER_RUN)]
        first = jnp.where(bits[0], 0, jnp.where(bits[1], 1, jnp.where(bits[2], 2, 3)))
        final = jnp.where(bits[3], 3, jnp.where(bits[2], 2, jnp.where(bits[1], 1, 0)))
        picks.append((g * PER_RUN + first, g * PER_RUN + final))
    own = [pattern[0, 0, r * PER_RUN + t] for t in range(PER_RUN)]
    count = own[0] + own[1] + own[2] + own[3]
    own_first = jnp.where(own[0] > 0, 0, jnp.where(own[1] > 0, 1, jnp.where(own[2] > 0, 2, 3)))
    own_final = jnp.where(own[3] > 0, 3, jnp.where(own[2] > 0, 2, jnp.where(own[1] > 0, 1, 0)))

    slab_copy.wait()
    limit = jnp.where(kept[0, 0, 0] > 0, fill[0, 0], 0)
    live = lax.broadcasted_iota(jnp.int32, (TILE, LANES), 0) < limit
    low = lax.broadcasted_iota(jnp.int32, (DEPTH, LANES), 1) < 64

    def swap(x):
        return pltpu.roll(x, 64, 1)

    for p, width in enumerate(PARTS):
        base = STARTS[p] // LANES * LANES
        piece = jnp.where(live, slab[:, base:base + LANES].astype(jnp.float32), 0.0)
        if width == 64:
            top, bottom = piece[:DEPTH], piece[DEPTH:]
            piece = jnp.where(low, top, swap(bottom)) if STARTS[p] == base else jnp.where(low, swap(top), bottom)
        right[p][c] = piece.astype(jnp.bfloat16)

    pl.semaphore_wait(barrier, len(mates) + 1)
    pl.semaphore_signal(greet_sem.at[0], inc=1, device_id=above, device_id_type=MESH)

    hop_list = [(d, u, h) for d in ("R", "L") for u in PIECES for h in range(1, HOPS[d][u] + 1)]
    number = {piece: i for i, piece in enumerate(hop_list)}

    def piece_view(direction, u, hops):
        tile = lax.rem(c + (TILES - 2 * hops if direction == "R" else 2 * hops), TILES)
        return right[u[0]].at[tile, pl.ds(u[1] * DEPTH, DEPTH)]

    def to_sibling(p, view):
        pltpu.make_async_remote_copy(
            src_ref=view, dst_ref=view, send_sem=pair_send.at[p], recv_sem=pair_recv.at[p],
            device_id=sibling, device_id_type=MESH).start()

    def hop_copy(direction, u, hop):
        view = piece_view(direction, u, hop - 1)
        return pltpu.make_async_remote_copy(
            src_ref=view, dst_ref=view, send_sem=ring_send.at[0 if direction == "R" else 1],
            recv_sem=ring_recv.at[number[direction, u, hop]], device_id=ring[direction], device_id_type=MESH)

    def arrive(direction, u, hop):
        view = piece_view(direction, u, hop)
        pltpu.make_async_copy(view, view, ring_recv.at[number[direction, u, hop]]).wait()
        return view

    def fill_stage(h):
        for slot, (tile, least) in enumerate(((own_first, 1), (own_final, 2))):
            weight = jnp.full((OWNED, TILE), jnp.where(count >= least, 1.0, 0.0), jnp.float32).astype(jnp.bfloat16)
            for half in range(2):
                first_row = pl.multiple_of(lax.rem(l + OFFSETS[2 * h + half], LAYERS) * OWNED, OWNED)
                piece = rows[tile, pl.ds(first_row, OWNED), :]
                left[h, r, slot, half * OWNED:(half + 1) * OWNED, :] = piece * weight

    def left_copy(h, way):
        view = left.at[h, r]
        return pltpu.make_async_remote_copy(
            src_ref=view, dst_ref=view, send_sem=left_send.at[h], recv_sem=left_recv.at[h, way],
            device_id=row_ring[way], device_id_type=MESH)

    def pass_copy(h, way):
        view = left.at[h, row_from[way], way]
        return pltpu.make_async_remote_copy(
            src_ref=view, dst_ref=view, send_sem=left_send.at[h], recv_sem=left_recv.at[h, 2],
            device_id=row_ring[way], device_id_type=MESH)

    have_rows, have_left, have_right = False, set(), set()
    for step in build_events():
        if step[0] == "send":
            _, direction, u, hop = step
            view = arrive(direction, u, hop - 1) if hop > 1 else None
            hop_copy(direction, u, hop).start()
            if view is not None:
                to_sibling(u[0], view)
        elif step[0] == "land":
            to_sibling(step[2][0], arrive(*step[1:]))
        elif step[0] == "greet":
            k = step[1]
            pl.semaphore_wait(greet_sem.at[k], 1 if k == 0 else 2)
            if k + 1 < len(GREET):
                for mate in (above, below):
                    pl.semaphore_signal(greet_sem.at[k + 1], inc=1, device_id=mate, device_id_type=MESH)
        elif step[0] == "share":
            to_sibling(step[1], right[step[1]].at[c])
        elif step[0] == "left":
            if not have_rows:
                have_rows = True
                for copy in tile_copies:
                    copy.wait()
            fill_stage(step[1])
            for way in range(2):
                left_copy(step[1], way).start()
        elif step[0] == "pass":
            for way in range(2):
                view = left.at[step[1], row_from[way]]
                pltpu.make_async_copy(view, view, left_recv.at[step[1], way]).wait()
                pass_copy(step[1], way).start()
        else:
            _, p, h = step
            if p not in have_right:
                have_right.add(p)
                view = right[p].at[pl.ds(0, TILES // 2)]
                pltpu.make_async_copy(view, view, pair_recv.at[p]).wait()
            if h not in have_left:
                have_left.add(h)
                view = left.at[h, 0]
                pltpu.make_async_copy(view, view, left_recv.at[h, 2]).wait()
            totals = [None, None]
            for g in range(RUNS):
                for slot in range(SLOTS):
                    tile = right[p][picks[g][slot]]
                    if PARTS[p] == LANES:
                        terms = [jnp.dot(left[h, g, slot], tile, preferred_element_type=jnp.float32)]
                    else:
                        terms = [
                            jnp.dot(left[h, g, slot, :, :DEPTH], tile, preferred_element_type=jnp.float32),
                            jnp.dot(left[h, g, slot, :, DEPTH:], tile, preferred_element_type=jnp.float32),
                        ]
                    for i, term in enumerate(terms):
                        totals[i] = term if totals[i] is None else totals[i] + term
            if PARTS[p] == LANES:
                partial[p][h] = totals[0].reshape(2, OWNED, LANES)
            else:
                in_low = totals[0] + swap(totals[1])
                in_high = swap(totals[0]) + totals[1]
                for half in range(2):
                    row = half * OWNED
                    partial[p][h, half] = jnp.where(
                        low[:OWNED // 2], in_low[row:row + OWNED // 2], in_high[row + OWNED // 2:row + OWNED])
            for half in range(2):
                k = 2 * h + half
                if OFFSETS[k] != 0:
                    pltpu.make_async_remote_copy(
                        src_ref=partial[p].at[h, half], dst_ref=landed[p].at[k],
                        send_sem=sum_send.at[p], recv_sem=sum_recv.at[p],
                        device_id=layer_mates[k], device_id_type=MESH).start()

    def drain(view, sem):
        pltpu.make_async_copy(view, view, sem).wait()

    for i in range(2):
        drain(right[0].at[pl.ds(0, TILES - 2)], ring_send.at[i])
    for h in range(STAGES):
        drain(left.at[h, pl.ds(0, RUNS - 1)], left_send.at[h])
    for p in range(count_parts):
        drain(right[p].at[pl.ds(0, TILES // 2)], pair_send.at[p])
    sums = []

    def finish(first_row, last_row, base, total):
        out_ref[first_row:last_row, base:base + LANES] = (
            total)

    for p in range(count_parts):
        drain(landed[p], sum_recv.at[p])
        total = partial[p][STAGES - 1, 1]
        for k in range(LAYERS - 1):
            total = total + landed[p][k]
        sums.append(total)
        base = STARTS[p] // LANES * LANES
        if PARTS[p] == LANES:
            finish(0, OWNED, base, total)
        elif STARTS[p] > base:
            one, two = sums[p - 1], sums[p]
            finish(0, OWNED // 2, base, jnp.where(low[:OWNED // 2], one, swap(two)))
            finish(OWNED // 2, OWNED, base, jnp.where(low[:OWNED // 2], swap(one), two))
    for p in range(count_parts):
        drain(landed[p], sum_send.at[p])


def body(iterate_rows, square_slab, row_pattern, slab_pattern, fill_counts, iterate_slab):
    in_hbm = pl.BlockSpec(memory_space=pltpu.HBM)
    dma = pltpu.SemaphoreType.DMA
    parts = len(PARTS)
    deep = [width // 64 for width in PARTS]
    product = pl.pallas_call(
        kernel,
        out_shape=jax.ShapeDtypeStruct((OWNED, TILE), jnp.float32),
        in_specs=[in_hbm] * 5,
        out_specs=pl.BlockSpec(memory_space=pltpu.VMEM),
        scratch_shapes=[
            pltpu.VMEM((PER_RUN, TILE, TILE), jnp.bfloat16),
            pltpu.VMEM((TILE, TILE), jnp.bfloat16),
            pltpu.SMEM((1, 1, TILES), jnp.int32),
            pltpu.SMEM((1, 1, 1), jnp.int32),
            pltpu.SMEM((1, 1), jnp.int32),
            pltpu.VMEM((STAGES, RUNS, SLOTS, STAGE_ROWS, TILE), jnp.bfloat16),
            dma((PER_RUN + 2,)), dma((3,)),
            dma((STAGES,)), dma((STAGES, 3)),
            dma((2,)), dma((len(PIECES) * (CHIPS - 1),)),
            dma((parts,)), dma((parts,)), dma((parts,)), dma((parts,)),
            pltpu.SemaphoreType.REGULAR((len(GREET),)),
        ]
        + [pltpu.VMEM((TILES, d * DEPTH, LANES), jnp.bfloat16) for d in deep]
        + [pltpu.VMEM((STAGES, 2, d * OWNED // 2, LANES), jnp.float32) for d in deep]
        + [pltpu.VMEM((LAYERS - 1, d * OWNED // 2, LANES), jnp.float32) for d in deep],
        compiler_params=pltpu.CompilerParams(
            collective_id=0, has_side_effects=True, vmem_limit_bytes=55000 << 10),
        name="sparse_product",
    )(iterate_rows, square_slab, row_pattern, slab_pattern, fill_counts)
    return 1.5 * iterate_slab - 0.5 * product


def solution(mesh):
    return jax.shard_map(
        body,
        mesh=mesh,
        in_specs=(
            P("layer", "col", "row"),
            P("layer", "col", "row"),
            P("layer", "col", None),
            P("layer", "col", "row"),
            P("layer", "col"),
            P(("col", "layer"), "row"),
        ),
        out_specs=P(("col", "layer"), "row"),
        check_vma=False,
    )
```

```python
import functools

import jax
import jax.numpy as jnp
from jax import lax
from jax.experimental import pallas as pl
from jax.experimental.pallas import tpu as pltpu
from jax.sharding import PartitionSpec as P

MESH = pl.DeviceIdType.MESH
TILE = 512
RUNS = 4
PER_RUN = 4
SLOTS = 2
TILES = 16
CHIPS = 8
LAYERS = 8
LANES = 128
PARTS = (128, 128, 64, 64, 64, 64)
STARTS = tuple(sum(PARTS[:p]) for p in range(len(PARTS)))
DEPTH = TILE // 2
PIECES = tuple((p, s) for p, width in enumerate(PARTS) for s in range(width // 64))
STAGES = 4
OWNED = TILE // LAYERS
STAGE_ROWS = TILE // STAGES
OFFSETS = (4, 3, 5, 2, 6, 1, 7, 0)
HOPS = {
    "R": {u: 4 - i % 2 for i, u in enumerate(PIECES)},
    "L": {u: 3 + i % 2 for i, u in enumerate(PIECES)},
}

SLOT = 1.4
LATENCY = 2.7
DEADLINES = (20, 23, 26, 32, 34, 37)
SEND_LEFT = (0.0, 0.0, 8.3, 13.8)
PASS_LEFT = (8.2, 13.7, 22.0, 30.2)
HAVE_LEFT = (17.0, 25.5, 34.0, 37.0)
GREET = (10.0, 14.0, 17.0, 19.0)


def ring_order(direction):
    hops = HOPS[direction]
    done = dict.fromkeys(hops, 0)
    ready = dict.fromkeys(hops, 0.0)
    order, now = [], 0.0
    while done != hops:
        left = [u for u in PIECES if done[u] < hops[u]]
        now = max(now, min(ready[u] for u in left))
        active = [u for u in left if ready[u] <= now]
        u = min(active, key=lambda u: (DEADLINES[u[0]] - (SLOT + LATENCY) * (hops[u] - done[u] - 1), u))
        done[u] += 1
        order.append((now, u, done[u]))
        now += SLOT
        ready[u] = now + LATENCY
    return order


def build_events():
    events = []
    complete = [0.0] * len(PARTS)
    for direction in ("R", "L"):
        arrived = {}
        for now, u, hop in ring_order(direction):
            events.append((max(now - SLOT, arrived.get(u, 0.0)), 1, now, ("send", direction, u, hop)))
            arrived[u] = now + SLOT + LATENCY
        for u, when in arrived.items():
            events.append((when, 0, when, ("land", direction, u, HOPS[direction][u])))
            complete[u[0]] = max(complete[u[0]], when)
    for p in range(len(PARTS)):
        events.append((1.5 * STARTS[p] / 64, 2, p, ("share", p)))
        for h in range(STAGES):
            events.append((max(complete[p] + 2.0, HAVE_LEFT[h]), 4, h, ("block", p, h)))
    for h in range(STAGES):
        events.append((SEND_LEFT[h], 3, h, ("left", h)))
        events.append((PASS_LEFT[h], 3, h, ("pass", h)))
    for k in range(len(GREET)):
        events.append((GREET[k], 3, k, ("greet", k)))
    return [e[3] for e in sorted(events, key=lambda e: e[:3])]


def kernel(
    rows_hbm, slab_hbm, pattern_hbm, kept_hbm, fill_hbm, out_ref,
    rows, slab, pattern, kept, fill, left, in_sem, scalar_sem, left_send, left_recv,
    ring_send, ring_recv, pair_send, pair_recv, sum_send, sum_recv, greet_sem, *buffers,
):
    count_parts = len(PARTS)
    right, partial, landed = (buffers[i * count_parts:(i + 1) * count_parts] for i in range(3))
    r, c, l = (lax.axis_index(name) for name in ("row", "col", "layer"))
    core = lax.rem(c, 2)
    sibling = (r, c + 1 - 2 * core, l)
    ring = {"R": (r, lax.rem(c + 2, TILES), l), "L": (r, lax.rem(c + TILES - 2, TILES), l)}
    row_ring = [(lax.rem(r + o, RUNS), c, l) for o in (1, RUNS - 1)]
    row_from = [lax.rem(r + o, RUNS) for o in (RUNS - 1, 1)]
    layer_mates = [(r, c, lax.rem(l + o, LAYERS)) for o in OFFSETS[:-1]]

    slab_copy = pltpu.make_async_copy(slab_hbm.at[0], slab, in_sem.at[PER_RUN])
    scalar_copies = [
        pltpu.make_async_copy(pattern_hbm, pattern, scalar_sem.at[0]),
        pltpu.make_async_copy(kept_hbm, kept, scalar_sem.at[1]),
        pltpu.make_async_copy(fill_hbm, fill, scalar_sem.at[2]),
    ]
    tile_copies = [
        pltpu.make_async_copy(rows_hbm.at[0, :, pl.ds(t * TILE, TILE)], rows.at[t], in_sem.at[t])
        for t in range(PER_RUN)
    ]
    for copy in scalar_copies + [slab_copy] + tile_copies:
        copy.start()

    barrier = pltpu.get_barrier_semaphore()
    above, below = (r, c, lax.rem(l + 1, LAYERS)), (r, c, lax.rem(l + LAYERS - 1, LAYERS))
    mates = row_ring + [ring["R"], ring["L"], sibling]
    for mate in mates + [below]:
        pl.semaphore_signal(barrier, inc=1, device_id=mate, device_id_type=MESH)

    for copy in scalar_copies:
        copy.wait()
    picks = []
    for g in range(RUNS):
        bits = [pattern[0, 0, g * PER_RUN + t] > 0 for t in range(PER_RUN)]
        first = jnp.where(bits[0], 0, jnp.where(bits[1], 1, jnp.where(bits[2], 2, 3)))
        final = jnp.where(bits[3], 3, jnp.where(bits[2], 2, jnp.where(bits[1], 1, 0)))
        picks.append((g * PER_RUN + first, g * PER_RUN + final))
    own = [pattern[0, 0, r * PER_RUN + t] for t in range(PER_RUN)]
    count = own[0] + own[1] + own[2] + own[3]
    own_first = jnp.where(own[0] > 0, 0, jnp.where(own[1] > 0, 1, jnp.where(own[2] > 0, 2, 3)))
    own_final = jnp.where(own[3] > 0, 3, jnp.where(own[2] > 0, 2, jnp.where(own[1] > 0, 1, 0)))

    slab_copy.wait()
    limit = jnp.where(kept[0, 0, 0] > 0, fill[0, 0], 0)
    live = lax.broadcasted_iota(jnp.int32, (TILE, LANES), 0) < limit
    low = lax.broadcasted_iota(jnp.int32, (DEPTH, LANES), 1) < 64

    def swap(x):
        return pltpu.roll(x, 64, 1)

    for p, width in enumerate(PARTS):
        base = STARTS[p] // LANES * LANES
        piece = jnp.where(live, slab[:, base:base + LANES].astype(jnp.float32), 0.0)
        if width == 64:
            top, bottom = piece[:DEPTH], piece[DEPTH:]
            piece = jnp.where(low, top, swap(bottom)) if STARTS[p] == base else jnp.where(low, swap(top), bottom)
        right[p][c] = piece.astype(jnp.bfloat16)

    pl.semaphore_wait(barrier, len(mates) + 1)
    pl.semaphore_signal(greet_sem.at[0], inc=1, device_id=above, device_id_type=MESH)

    hop_list = [(d, u, h) for d in ("R", "L") for u in PIECES for h in range(1, HOPS[d][u] + 1)]
    number = {piece: i for i, piece in enumerate(hop_list)}

    def piece_view(direction, u, hops):
        tile = lax.rem(c + (TILES - 2 * hops if direction == "R" else 2 * hops), TILES)
        return right[u[0]].at[tile, pl.ds(u[1] * DEPTH, DEPTH)]

    def to_sibling(p, view):
        pltpu.make_async_remote_copy(
            src_ref=view, dst_ref=view, send_sem=pair_send.at[p], recv_sem=pair_recv.at[p],
            device_id=sibling, device_id_type=MESH).start()

    def hop_copy(direction, u, hop):
        view = piece_view(direction, u, hop - 1)
        return pltpu.make_async_remote_copy(
            src_ref=view, dst_ref=view, send_sem=ring_send.at[0 if direction == "R" else 1],
            recv_sem=ring_recv.at[number[direction, u, hop]], device_id=ring[direction], device_id_type=MESH)

    def arrive(direction, u, hop):
        view = piece_view(direction, u, hop)
        pltpu.make_async_copy(view, view, ring_recv.at[number[direction, u, hop]]).wait()
        return view

    def fill_stage(h):
        for slot, (tile, least) in enumerate(((own_first, 1), (own_final, 2))):
            weight = jnp.full((OWNED, TILE), jnp.where(count >= least, 1.0, 0.0), jnp.float32).astype(jnp.bfloat16)
            for half in range(2):
                first_row = pl.multiple_of(lax.rem(l + OFFSETS[2 * h + half], LAYERS) * OWNED, OWNED)
                piece = rows[tile, pl.ds(first_row, OWNED), :]
                left[h, r, slot, half * OWNED:(half + 1) * OWNED, :] = piece * weight

    def left_copy(h, way):
        view = left.at[h, r]
        return pltpu.make_async_remote_copy(
            src_ref=view, dst_ref=view, send_sem=left_send.at[h], recv_sem=left_recv.at[h, way],
            device_id=row_ring[way], device_id_type=MESH)

    def pass_copy(h, way):
        view = left.at[h, row_from[way], way]
        return pltpu.make_async_remote_copy(
            src_ref=view, dst_ref=view, send_sem=left_send.at[h], recv_sem=left_recv.at[h, 2],
            device_id=row_ring[way], device_id_type=MESH)

    have_rows, have_left, have_right = False, set(), set()
    for step in build_events():
        if step[0] == "send":
            _, direction, u, hop = step
            view = arrive(direction, u, hop - 1) if hop > 1 else None
            hop_copy(direction, u, hop).start()
            if view is not None:
                to_sibling(u[0], view)
        elif step[0] == "land":
            to_sibling(step[2][0], arrive(*step[1:]))
        elif step[0] == "greet":
            k = step[1]
            pl.semaphore_wait(greet_sem.at[k], 1 if k == 0 else 2)
            if k + 1 < len(GREET):
                for mate in (above, below):
                    pl.semaphore_signal(greet_sem.at[k + 1], inc=1, device_id=mate, device_id_type=MESH)
        elif step[0] == "share":
            to_sibling(step[1], right[step[1]].at[c])
        elif step[0] == "left":
            if not have_rows:
                have_rows = True
                for copy in tile_copies:
                    copy.wait()
            fill_stage(step[1])
            for way in range(2):
                left_copy(step[1], way).start()
        elif step[0] == "pass":
            for way in range(2):
                view = left.at[step[1], row_from[way]]
                pltpu.make_async_copy(view, view, left_recv.at[step[1], way]).wait()
                pass_copy(step[1], way).start()
        else:
            _, p, h = step
            if p not in have_right:
                have_right.add(p)
                view = right[p].at[pl.ds(0, TILES // 2)]
                pltpu.make_async_copy(view, view, pair_recv.at[p]).wait()
            if h not in have_left:
                have_left.add(h)
                view = left.at[h, 0]
                pltpu.make_async_copy(view, view, left_recv.at[h, 2]).wait()
            totals = [None, None]
            for g in range(RUNS):
                for slot in range(SLOTS):
                    tile = right[p][picks[g][slot]]
                    if PARTS[p] == LANES:
                        terms = [jnp.dot(left[h, g, slot], tile, preferred_element_type=jnp.float32)]
                    else:
                        terms = [
                            jnp.dot(left[h, g, slot, :, :DEPTH], tile, preferred_element_type=jnp.float32),
                            jnp.dot(left[h, g, slot, :, DEPTH:], tile, preferred_element_type=jnp.float32),
                        ]
                    for i, term in enumerate(terms):
                        totals[i] = term if totals[i] is None else totals[i] + term
            if PARTS[p] == LANES:
                partial[p][h] = totals[0].reshape(2, OWNED, LANES)
            else:
                in_low = totals[0] + swap(totals[1])
                in_high = swap(totals[0]) + totals[1]
                for half in range(2):
                    row = half * OWNED
                    partial[p][h, half] = jnp.where(
                        low[:OWNED // 2], in_low[row:row + OWNED // 2], in_high[row + OWNED // 2:row + OWNED])
            for half in range(2):
                k = 2 * h + half
                if OFFSETS[k] != 0:
                    pltpu.make_async_remote_copy(
                        src_ref=partial[p].at[h, half], dst_ref=landed[p].at[k],
                        send_sem=sum_send.at[p], recv_sem=sum_recv.at[p],
                        device_id=layer_mates[k], device_id_type=MESH).start()

    def drain(view, sem):
        pltpu.make_async_copy(view, view, sem).wait()

    for i in range(2):
        drain(right[0].at[pl.ds(0, TILES - 2)], ring_send.at[i])
    for h in range(STAGES):
        drain(left.at[h, pl.ds(0, RUNS - 1)], left_send.at[h])
    for p in range(count_parts):
        drain(right[p].at[pl.ds(0, TILES // 2)], pair_send.at[p])
    sums = []

    def finish(first_row, last_row, base, total):
        out_ref[first_row:last_row, base:base + LANES] = (
            total)

    for p in range(count_parts):
        drain(landed[p], sum_recv.at[p])
        total = partial[p][STAGES - 1, 1]
        for k in range(LAYERS - 1):
            total = total + landed[p][k]
        sums.append(total)
        base = STARTS[p] // LANES * LANES
        if PARTS[p] == LANES:
            finish(0, OWNED, base, total)
        elif STARTS[p] > base:
            one, two = sums[p - 1], sums[p]
            finish(0, OWNED // 2, base, jnp.where(low[:OWNED // 2], one, swap(two)))
            finish(OWNED // 2, OWNED, base, jnp.where(low[:OWNED // 2], swap(one), two))
    for p in range(count_parts):
        drain(landed[p], sum_send.at[p])


def body(iterate_rows, square_slab, row_pattern, slab_pattern, fill_counts, iterate_slab):
    in_hbm = pl.BlockSpec(memory_space=pltpu.HBM)
    dma = pltpu.SemaphoreType.DMA
    parts = len(PARTS)
    deep = [width // 64 for width in PARTS]
    product = pl.pallas_call(
        kernel,
        out_shape=jax.ShapeDtypeStruct((OWNED, TILE), jnp.float32),
        in_specs=[in_hbm] * 5,
        out_specs=pl.BlockSpec(memory_space=pltpu.VMEM),
        scratch_shapes=[
            pltpu.VMEM((PER_RUN, TILE, TILE), jnp.bfloat16),
            pltpu.VMEM((TILE, TILE), jnp.bfloat16),
            pltpu.SMEM((1, 1, TILES), jnp.int32),
            pltpu.SMEM((1, 1, 1), jnp.int32),
            pltpu.SMEM((1, 1), jnp.int32),
            pltpu.VMEM((STAGES, RUNS, SLOTS, STAGE_ROWS, TILE), jnp.bfloat16),
            dma((PER_RUN + 2,)), dma((3,)),
            dma((STAGES,)), dma((STAGES, 3)),
            dma((2,)), dma((len(PIECES) * (CHIPS - 1),)),
            dma((parts,)), dma((parts,)), dma((parts,)), dma((parts,)),
            pltpu.SemaphoreType.REGULAR((len(GREET),)),
        ]
        + [pltpu.VMEM((TILES, d * DEPTH, LANES), jnp.bfloat16) for d in deep]
        + [pltpu.VMEM((STAGES, 2, d * OWNED // 2, LANES), jnp.float32) for d in deep]
        + [pltpu.VMEM((LAYERS - 1, d * OWNED // 2, LANES), jnp.float32) for d in deep],
        compiler_params=pltpu.CompilerParams(
            collective_id=0, has_side_effects=True, vmem_limit_bytes=55000 << 10),
        name="sparse_product",
    )(iterate_rows, square_slab, row_pattern, slab_pattern, fill_counts)
    return 1.5 * iterate_slab - 0.5 * product


def solution(mesh):
    return jax.shard_map(
        body,
        mesh=mesh,
        in_specs=(
            P("layer", "col", "row"),
            P("layer", "col", "row"),
            P("layer", "col", None),
            P("layer", "col", "row"),
            P("layer", "col"),
            P(("col", "layer"), "row"),
        ),
        out_specs=P(("col", "layer"), "row"),
        check_vma=False,
    )
```

```python
import functools

import jax
import jax.numpy as jnp
from jax import lax
from jax.experimental import pallas as pl
from jax.experimental.pallas import tpu as pltpu
from jax.sharding import PartitionSpec as P

MESH = pl.DeviceIdType.MESH
TILE = 512
RUNS = 4
PER_RUN = 4
SLOTS = 2
TILES = 16
CHIPS = 8
LAYERS = 8
LANES = 128
PARTS = (128, 128, 64, 64, 64, 64)
STARTS = tuple(sum(PARTS[:p]) for p in range(len(PARTS)))
DEPTH = TILE // 2
PIECES = tuple((p, s) for p, width in enumerate(PARTS) for s in range(width // 64))
STAGES = 4
OWNED = TILE // LAYERS
STAGE_ROWS = TILE // STAGES
OFFSETS = (4, 3, 5, 2, 6, 1, 7, 0)
HOPS = {
    "R": {u: 4 - i % 2 for i, u in enumerate(PIECES)},
    "L": {u: 3 + i % 2 for i, u in enumerate(PIECES)},
}

SLOT = 1.4
LATENCY = 2.7
DEADLINES = (20, 23, 26, 32, 34, 37)
SEND_LEFT = (0.0, 0.0, 8.3, 13.8)
PASS_LEFT = (8.2, 13.7, 22.0, 30.2)
HAVE_LEFT = (17.0, 25.5, 34.0, 37.0)
GREET = (5.5, 11.0, 16.0, 20.5)


def ring_order(direction):
    hops = HOPS[direction]
    done = dict.fromkeys(hops, 0)
    ready = dict.fromkeys(hops, 0.0)
    order, now = [], 0.0
    while done != hops:
        left = [u for u in PIECES if done[u] < hops[u]]
        now = max(now, min(ready[u] for u in left))
        active = [u for u in left if ready[u] <= now]
        u = min(active, key=lambda u: (DEADLINES[u[0]] - (SLOT + LATENCY) * (hops[u] - done[u] - 1), u))
        done[u] += 1
        order.append((now, u, done[u]))
        now += SLOT
        ready[u] = now + LATENCY
    return order


def build_events():
    events = []
    complete = [0.0] * len(PARTS)
    for direction in ("R", "L"):
        arrived = {}
        for now, u, hop in ring_order(direction):
            events.append((max(now - SLOT, arrived.get(u, 0.0)), 1, now, ("send", direction, u, hop)))
            arrived[u] = now + SLOT + LATENCY
        for u, when in arrived.items():
            events.append((when, 0, when, ("land", direction, u, HOPS[direction][u])))
            complete[u[0]] = max(complete[u[0]], when)
    for p in range(len(PARTS)):
        events.append((1.5 * STARTS[p] / 64, 2, p, ("share", p)))
        for h in range(STAGES):
            events.append((max(complete[p] + 2.0, HAVE_LEFT[h]), 4, h, ("block", p, h)))
    for h in range(STAGES):
        events.append((SEND_LEFT[h], 3, h, ("left", h)))
        events.append((PASS_LEFT[h], 3, h, ("pass", h)))
    for k in range(len(GREET)):
        events.append((GREET[k], 3, k, ("greet", k)))
    return [e[3] for e in sorted(events, key=lambda e: e[:3])]


def kernel(
    rows_hbm, slab_hbm, pattern_hbm, kept_hbm, fill_hbm, out_ref,
    rows, slab, pattern, kept, fill, left, in_sem, scalar_sem, left_send, left_recv,
    ring_send, ring_recv, pair_send, pair_recv, sum_send, sum_recv, greet_sem, *buffers,
):
    count_parts = len(PARTS)
    right, partial, landed = (buffers[i * count_parts:(i + 1) * count_parts] for i in range(3))
    r, c, l = (lax.axis_index(name) for name in ("row", "col", "layer"))
    core = lax.rem(c, 2)
    sibling = (r, c + 1 - 2 * core, l)
    ring = {"R": (r, lax.rem(c + 2, TILES), l), "L": (r, lax.rem(c + TILES - 2, TILES), l)}
    row_ring = [(lax.rem(r + o, RUNS), c, l) for o in (1, RUNS - 1)]
    row_from = [lax.rem(r + o, RUNS) for o in (RUNS - 1, 1)]
    layer_mates = [(r, c, lax.rem(l + o, LAYERS)) for o in OFFSETS[:-1]]

    slab_copy = pltpu.make_async_copy(slab_hbm.at[0], slab, in_sem.at[PER_RUN])
    scalar_copies = [
        pltpu.make_async_copy(pattern_hbm, pattern, scalar_sem.at[0]),
        pltpu.make_async_copy(kept_hbm, kept, scalar_sem.at[1]),
        pltpu.make_async_copy(fill_hbm, fill, scalar_sem.at[2]),
    ]
    tile_copies = [
        pltpu.make_async_copy(rows_hbm.at[0, :, pl.ds(t * TILE, TILE)], rows.at[t], in_sem.at[t])
        for t in range(PER_RUN)
    ]
    for copy in scalar_copies + [slab_copy] + tile_copies:
        copy.start()

    barrier = pltpu.get_barrier_semaphore()
    above, below = (r, c, lax.rem(l + 1, LAYERS)), (r, c, lax.rem(l + LAYERS - 1, LAYERS))
    mates = row_ring + [ring["R"], ring["L"], sibling]
    for mate in mates + [below]:
        pl.semaphore_signal(barrier, inc=1, device_id=mate, device_id_type=MESH)

    for copy in scalar_copies:
        copy.wait()
    picks = []
    for g in range(RUNS):
        bits = [pattern[0, 0, g * PER_RUN + t] > 0 for t in range(PER_RUN)]
        first = jnp.where(bits[0], 0, jnp.where(bits[1], 1, jnp.where(bits[2], 2, 3)))
        final = jnp.where(bits[3], 3, jnp.where(bits[2], 2, jnp.where(bits[1], 1, 0)))
        picks.append((g * PER_RUN + first, g * PER_RUN + final))
    own = [pattern[0, 0, r * PER_RUN + t] for t in range(PER_RUN)]
    count = own[0] + own[1] + own[2] + own[3]
    own_first = jnp.where(own[0] > 0, 0, jnp.where(own[1] > 0, 1, jnp.where(own[2] > 0, 2, 3)))
    own_final = jnp.where(own[3] > 0, 3, jnp.where(own[2] > 0, 2, jnp.where(own[1] > 0, 1, 0)))

    slab_copy.wait()
    limit = jnp.where(kept[0, 0, 0] > 0, fill[0, 0], 0)
    live = lax.broadcasted_iota(jnp.int32, (TILE, LANES), 0) < limit
    low = lax.broadcasted_iota(jnp.int32, (DEPTH, LANES), 1) < 64

    def swap(x):
        return pltpu.roll(x, 64, 1)

    for p, width in enumerate(PARTS):
        base = STARTS[p] // LANES * LANES
        piece = jnp.where(live, slab[:, base:base + LANES].astype(jnp.float32), 0.0)
        if width == 64:
            top, bottom = piece[:DEPTH], piece[DEPTH:]
            piece = jnp.where(low, top, swap(bottom)) if STARTS[p] == base else jnp.where(low, swap(top), bottom)
        right[p][c] = piece.astype(jnp.bfloat16)

    pl.semaphore_wait(barrier, len(mates) + 1)
    pl.semaphore_signal(greet_sem.at[0], inc=1, device_id=above, device_id_type=MESH)

    hop_list = [(d, u, h) for d in ("R", "L") for u in PIECES for h in range(1, HOPS[d][u] + 1)]
    number = {piece: i for i, piece in enumerate(hop_list)}

    def piece_view(direction, u, hops):
        tile = lax.rem(c + (TILES - 2 * hops if direction == "R" else 2 * hops), TILES)
        return right[u[0]].at[tile, pl.ds(u[1] * DEPTH, DEPTH)]

    def to_sibling(p, view):
        pltpu.make_async_remote_copy(
            src_ref=view, dst_ref=view, send_sem=pair_send.at[p], recv_sem=pair_recv.at[p],
            device_id=sibling, device_id_type=MESH).start()

    def hop_copy(direction, u, hop):
        view = piece_view(direction, u, hop - 1)
        return pltpu.make_async_remote_copy(
            src_ref=view, dst_ref=view, send_sem=ring_send.at[0 if direction == "R" else 1],
            recv_sem=ring_recv.at[number[direction, u, hop]], device_id=ring[direction], device_id_type=MESH)

    def arrive(direction, u, hop):
        view = piece_view(direction, u, hop)
        pltpu.make_async_copy(view, view, ring_recv.at[number[direction, u, hop]]).wait()
        return view

    def fill_stage(h):
        for slot, (tile, least) in enumerate(((own_first, 1), (own_final, 2))):
            weight = jnp.full((OWNED, TILE), jnp.where(count >= least, 1.0, 0.0), jnp.float32).astype(jnp.bfloat16)
            for half in range(2):
                first_row = pl.multiple_of(lax.rem(l + OFFSETS[2 * h + half], LAYERS) * OWNED, OWNED)
                piece = rows[tile, pl.ds(first_row, OWNED), :]
                left[h, r, slot, half * OWNED:(half + 1) * OWNED, :] = piece * weight

    def left_copy(h, way):
        view = left.at[h, r]
        return pltpu.make_async_remote_copy(
            src_ref=view, dst_ref=view, send_sem=left_send.at[h], recv_sem=left_recv.at[h, way],
            device_id=row_ring[way], device_id_type=MESH)

    def pass_copy(h, way):
        view = left.at[h, row_from[way], way]
        return pltpu.make_async_remote_copy(
            src_ref=view, dst_ref=view, send_sem=left_send.at[h], recv_sem=left_recv.at[h, 2],
            device_id=row_ring[way], device_id_type=MESH)

    have_rows, have_left, have_right = False, set(), set()
    for step in build_events():
        if step[0] == "send":
            _, direction, u, hop = step
            view = arrive(direction, u, hop - 1) if hop > 1 else None
            hop_copy(direction, u, hop).start()
            if view is not None:
                to_sibling(u[0], view)
        elif step[0] == "land":
            to_sibling(step[2][0], arrive(*step[1:]))
        elif step[0] == "greet":
            k = step[1]
            pl.semaphore_wait(greet_sem.at[k], 1 if k == 0 else 2)
            if k + 1 < len(GREET):
                for mate in (above, below):
                    pl.semaphore_signal(greet_sem.at[k + 1], inc=1, device_id=mate, device_id_type=MESH)
        elif step[0] == "share":
            to_sibling(step[1], right[step[1]].at[c])
        elif step[0] == "left":
            if not have_rows:
                have_rows = True
                for copy in tile_copies:
                    copy.wait()
            fill_stage(step[1])
            for way in range(2):
                left_copy(step[1], way).start()
        elif step[0] == "pass":
            for way in range(2):
                view = left.at[step[1], row_from[way]]
                pltpu.make_async_copy(view, view, left_recv.at[step[1], way]).wait()
                pass_copy(step[1], way).start()
        else:
            _, p, h = step
            if p not in have_right:
                have_right.add(p)
                view = right[p].at[pl.ds(0, TILES // 2)]
                pltpu.make_async_copy(view, view, pair_recv.at[p]).wait()
            if h not in have_left:
                have_left.add(h)
                view = left.at[h, 0]
                pltpu.make_async_copy(view, view, left_recv.at[h, 2]).wait()
            totals = [None, None]
            for g in range(RUNS):
                for slot in range(SLOTS):
                    tile = right[p][picks[g][slot]]
                    if PARTS[p] == LANES:
                        terms = [jnp.dot(left[h, g, slot], tile, preferred_element_type=jnp.float32)]
                    else:
                        terms = [
                            jnp.dot(left[h, g, slot, :, :DEPTH], tile, preferred_element_type=jnp.float32),
                            jnp.dot(left[h, g, slot, :, DEPTH:], tile, preferred_element_type=jnp.float32),
                        ]
                    for i, term in enumerate(terms):
                        totals[i] = term if totals[i] is None else totals[i] + term
            if PARTS[p] == LANES:
                partial[p][h] = totals[0].reshape(2, OWNED, LANES)
            else:
                in_low = totals[0] + swap(totals[1])
                in_high = swap(totals[0]) + totals[1]
                for half in range(2):
                    row = half * OWNED
                    partial[p][h, half] = jnp.where(
                        low[:OWNED // 2], in_low[row:row + OWNED // 2], in_high[row + OWNED // 2:row + OWNED])
            for half in range(2):
                k = 2 * h + half
                if OFFSETS[k] != 0:
                    pltpu.make_async_remote_copy(
                        src_ref=partial[p].at[h, half], dst_ref=landed[p].at[k],
                        send_sem=sum_send.at[p], recv_sem=sum_recv.at[p],
                        device_id=layer_mates[k], device_id_type=MESH).start()

    def drain(view, sem):
        pltpu.make_async_copy(view, view, sem).wait()

    for i in range(2):
        drain(right[0].at[pl.ds(0, TILES - 2)], ring_send.at[i])
    for h in range(STAGES):
        drain(left.at[h, pl.ds(0, RUNS - 1)], left_send.at[h])
    for p in range(count_parts):
        drain(right[p].at[pl.ds(0, TILES // 2)], pair_send.at[p])
    sums = []

    def finish(first_row, last_row, base, total):
        out_ref[first_row:last_row, base:base + LANES] = (
            total)

    for p in range(count_parts):
        drain(landed[p], sum_recv.at[p])
        total = partial[p][STAGES - 1, 1]
        for k in range(LAYERS - 1):
            total = total + landed[p][k]
        sums.append(total)
        base = STARTS[p] // LANES * LANES
        if PARTS[p] == LANES:
            finish(0, OWNED, base, total)
        elif STARTS[p] > base:
            one, two = sums[p - 1], sums[p]
            finish(0, OWNED // 2, base, jnp.where(low[:OWNED // 2], one, swap(two)))
            finish(OWNED // 2, OWNED, base, jnp.where(low[:OWNED // 2], swap(one), two))
    for p in range(count_parts):
        drain(landed[p], sum_send.at[p])


def body(iterate_rows, square_slab, row_pattern, slab_pattern, fill_counts, iterate_slab):
    in_hbm = pl.BlockSpec(memory_space=pltpu.HBM)
    dma = pltpu.SemaphoreType.DMA
    parts = len(PARTS)
    deep = [width // 64 for width in PARTS]
    product = pl.pallas_call(
        kernel,
        out_shape=jax.ShapeDtypeStruct((OWNED, TILE), jnp.float32),
        in_specs=[in_hbm] * 5,
        out_specs=pl.BlockSpec(memory_space=pltpu.VMEM),
        scratch_shapes=[
            pltpu.VMEM((PER_RUN, TILE, TILE), jnp.bfloat16),
            pltpu.VMEM((TILE, TILE), jnp.bfloat16),
            pltpu.SMEM((1, 1, TILES), jnp.int32),
            pltpu.SMEM((1, 1, 1), jnp.int32),
            pltpu.SMEM((1, 1), jnp.int32),
            pltpu.VMEM((STAGES, RUNS, SLOTS, STAGE_ROWS, TILE), jnp.bfloat16),
            dma((PER_RUN + 2,)), dma((3,)),
            dma((STAGES,)), dma((STAGES, 3)),
            dma((2,)), dma((len(PIECES) * (CHIPS - 1),)),
            dma((parts,)), dma((parts,)), dma((parts,)), dma((parts,)),
            pltpu.SemaphoreType.REGULAR((len(GREET),)),
        ]
        + [pltpu.VMEM((TILES, d * DEPTH, LANES), jnp.bfloat16) for d in deep]
        + [pltpu.VMEM((STAGES, 2, d * OWNED // 2, LANES), jnp.float32) for d in deep]
        + [pltpu.VMEM((LAYERS - 1, d * OWNED // 2, LANES), jnp.float32) for d in deep],
        compiler_params=pltpu.CompilerParams(
            collective_id=0, has_side_effects=True, vmem_limit_bytes=55000 << 10),
        name="sparse_product",
    )(iterate_rows, square_slab, row_pattern, slab_pattern, fill_counts)
    return 1.5 * iterate_slab - 0.5 * product


def solution(mesh):
    return jax.shard_map(
        body,
        mesh=mesh,
        in_specs=(
            P("layer", "col", "row"),
            P("layer", "col", "row"),
            P("layer", "col", None),
            P("layer", "col", "row"),
            P("layer", "col"),
            P(("col", "layer"), "row"),
        ),
        out_specs=P(("col", "layer"), "row"),
        check_vma=False,
    )
```
